256 devices in a mesh: ka: 128 (over z, x_lo, y, core), aux: 2 (over x_hi).
Axes of the slice: x: 4 (x_hi: 2, x_lo: 2; x = x_hi * 2 + x_lo), y: 4, z: 8, core: 2. Of those that a mesh axis runs over, the one named last changes fastest.
Arguments:
- coefficients: bfloat16 [128, 4096, 128], P('ka'), may hold values from -2.09375 to 2.09375
- triple: bfloat16 [64, 2, 64, 768], P('aux'), may hold values from -0.5 to 0.5
- neighbors: int32 [64, 2], P('aux'), may hold values from 0 to 63
- w_screened: bfloat16 [128, 768, 1536], P('ka', 'aux'), as said below
- partner: int32 [2, 128], replicated, may hold values from 0 to 127, each once within a row
- q_ids: int32 [2], replicated, may hold values from 0 to 127
Outputs:
- sigma: float32 [128, 64, 128], P('ka', 'aux')
The draws below stay inside these ranges and needn't reach their ends.
Inputs may be any that keep to these rules, and one draw needn't show every extreme that they name: Each stored w_screened is Hermitian: its real block is symmetric and its imaginary block antisymmetric.
All inputs are finite; a program needn't handle non-finite values.
Results may differ from the reference program's by a relative error of at most 0.0085.
Values may be sent and summed in bfloat16 or wider, within the bound.
No kernel may reach another device: no remote copies, remote signals or barrier semaphores. Data moves between devices by JAX's collectives and lax.ppermute only.
A program may use at most 128 MiB of HBM per device.

```python
import math
import jax
import jax.numpy as jnp
from jax import lax

CELL_ATOMS = 64
ORBITALS_PER_ATOM = 64
AUX_ATOM = 12
SIGMA_BANDS = 64
OCCUPIED_BANDS = 16
NEIGH = 2
TRANSFERS = 2
ORB = 4096
NAUX = 768
NK = 128
QPTS = 128


def draw_w_screened(key, part):
    keys = jax.random.split(jax.random.fold_in(key, 31), QPTS)

    def single(subkey):
        first, second, third, fourth = jax.random.split(subkey, 4)
        sym_base = jax.random.normal(first, (NAUX, NAUX), jnp.float32)
        anti_base = jax.random.normal(second, (NAUX, NAUX), jnp.float32)
        magnitude = jax.random.uniform(third, (NAUX,), jnp.float32, 0.5, 1.5)
        signs = jnp.where(jax.random.bernoulli(fourth, 0.5, (NAUX,)), 1.0, -1.0)
        real_block = 0.6 * (sym_base + sym_base.T) / jnp.sqrt(2.0 * NAUX) + jnp.diag(magnitude * signs)
        imag_block = 0.6 * (anti_base - anti_base.T) / jnp.sqrt(2.0 * NAUX)
        return jnp.concatenate([real_block, imag_block], axis=1)
    return lax.map(single, keys).astype(jnp.bfloat16)


def with_ends(entries, rng, smallest, top_value):
    spot = [jax.random.randint(jax.random.fold_in(rng, axis), (), 0, length) for axis, length in enumerate(entries.shape)]
    longest = entries.shape.index(max(entries.shape))
    neighbour = spot[:longest] + [(spot[longest] + 1) % entries.shape[longest]] + spot[longest + 1:]
    return entries.at[tuple(spot)].set(smallest).at[tuple(neighbour)].set(top_value)


def levels(stream_key, extent, shards, smallest, largest):
    factor_of, own = 1.0, jax.random.fold_in(stream_key, 6)
    for axis_at, parts in shards:
        steps = jnp.exp(jax.random.uniform(jax.random.fold_in(own, axis_at), (parts,), jnp.float32, smallest / len(shards), largest / len(shards)))
        factor_of = factor_of * jnp.repeat(steps, extent[axis_at] // parts).reshape([-1 if axis == axis_at else 1 for axis in range(len(extent))])
    return factor_of


def bell_draw(stream_key, extent, deviation, most, pieces=(), kind=jnp.bfloat16):
    drawn = jax.random.normal(stream_key, extent, jnp.float32) * deviation
    if len(pieces) > 0:
        drawn = levels(stream_key, extent, pieces, -0.22, 0.18) * drawn
    return jnp.clip(drawn, min=-most, max=most).astype(kind)


def setup_inputs(seed: int = 0) -> dict:
    streams_of = jax.random.split(jax.random.key(seed), 7)
    coefficients = bell_draw(streams_of[0], (NK, ORB, 2 * SIGMA_BANDS), 0.35, 2.09375, ((0, 128),))
    triple = bell_draw(streams_of[1], (CELL_ATOMS, NEIGH, ORBITALS_PER_ATOM, AUX_ATOM * ORBITALS_PER_ATOM), (ORBITALS_PER_ATOM * NEIGH) ** -0.5, 0.5, ((0, 2),))
    neighbors = with_ends(jax.random.randint(streams_of[2], (CELL_ATOMS, NEIGH), 0, CELL_ATOMS), jax.random.fold_in(streams_of[2], 1), 0, CELL_ATOMS - 1).astype(jnp.int32)
    w_screened = draw_w_screened(jax.random.fold_in(streams_of[6], 71), 0)
    partner = jax.vmap(lambda own: jax.random.permutation(own, NK))(jax.random.split(streams_of[4], TRANSFERS)).reshape((TRANSFERS, NK)).astype(jnp.int32)
    q_ids = jax.random.randint(streams_of[5], (TRANSFERS,), 0, QPTS).astype(jnp.int32)
    return {"coefficients": coefficients, "triple": triple, "neighbors": neighbors, "w_screened": w_screened, "partner": partner, "q_ids": q_ids}


def reference(coefficients, triple, neighbors, w_screened, partner, q_ids):
    band_count = SIGMA_BANDS
    prefactor = -1.0 / math.sqrt(TRANSFERS * NAUX * OCCUPIED_BANDS)
    distant_coef_gathered = jnp.concatenate([coefficients[:, :, :OCCUPIED_BANDS], coefficients[:, :, SIGMA_BANDS:SIGMA_BANDS + OCCUPIED_BANDS]], axis=2)
    triple_wide = triple.astype(jnp.float32)

    def each_kpoint_values(kpoint_index):
        home_coefficients = coefficients[kpoint_index].reshape(CELL_ATOMS, ORBITALS_PER_ATOM, 2 * SIGMA_BANDS).astype(jnp.float32)
        blocks = jnp.zeros((2 * SIGMA_BANDS, 2 * SIGMA_BANDS), jnp.float32)
        for momentum_transfer in range(TRANSFERS):
            distant_coefficients = distant_coef_gathered[partner[momentum_transfer, kpoint_index]].reshape(CELL_ATOMS, ORBITALS_PER_ATOM, 2 * OCCUPIED_BANDS)
            neighbour_coef = jnp.take(distant_coefficients, neighbors, axis=0).astype(jnp.float32)
            pair_half = jnp.einsum('cjoy,cjox->cyx', neighbour_coef, triple_wide).astype(jnp.bfloat16)
            pair_half = pair_half.reshape(CELL_ATOMS, 2 * OCCUPIED_BANDS, AUX_ATOM, ORBITALS_PER_ATOM).astype(jnp.float32)
            combos = jnp.einsum('cix,cyai->cayx', home_coefficients, pair_half)
            real_part = combos[..., :OCCUPIED_BANDS, :band_count] + combos[..., OCCUPIED_BANDS:, band_count:]
            imag_part = combos[..., OCCUPIED_BANDS:, :band_count] - combos[..., :OCCUPIED_BANDS, band_count:]
            products = jnp.concatenate([real_part, imag_part], axis=-1).astype(jnp.bfloat16)
            products = products.reshape(NAUX, OCCUPIED_BANDS, 2 * SIGMA_BANDS)
            rotated = jnp.concatenate([-products[..., band_count:], products[..., :band_count]], axis=-1)
            stacked = jnp.concatenate([products, rotated], axis=0).reshape(2 * NAUX, OCCUPIED_BANDS * 2 * SIGMA_BANDS)
            weights = w_screened[q_ids[momentum_transfer]]
            screened = jnp.dot(weights, stacked, preferred_element_type=jnp.float32).astype(jnp.bfloat16)
            screened = screened.reshape(NAUX * OCCUPIED_BANDS, 2 * SIGMA_BANDS)
            left_side = products.reshape(NAUX * OCCUPIED_BANDS, 2 * SIGMA_BANDS)
            blocks = blocks + lax.dot_general(left_side, screened, (((0,), (0,)), ((), ())), preferred_element_type=jnp.float32)
        sigma_real = blocks[:band_count, :band_count] + blocks[band_count:, band_count:]
        sigma_imag = blocks[:band_count, band_count:] - blocks[band_count:, :band_count]
        return prefactor * jnp.concatenate([sigma_real, sigma_imag], axis=-1)
    return lax.map(each_kpoint_values, jnp.arange(NK, dtype=jnp.int32))
```

```python
import math

import jax
import jax.numpy as jnp
from jax import lax
from jax.experimental import pallas as pl
from jax.experimental.pallas import tpu as pltpu
from jax.sharding import Mesh
from jax.sharding import PartitionSpec as P

ATOMS = 64
ORBS = 64
AUX_ATOM = 12
BANDS = 64
OCC = 16
TRANSFERS = 2
NAUX = ATOMS * AUX_ATOM
HALF = NAUX // 2
BF = jnp.bfloat16
F32 = jnp.float32
KA = ("z", "xl", "y", "core")
PEERS = 128
FAR_TILES = 64
W_TILES = HALF * NAUX // (16 * 128)
PREFACTOR = -1.0 / math.sqrt(TRANSFERS * NAUX * OCC)
VMEM = 56 * 2**20


def dot(a, b):
    return jnp.dot(a, b, preferred_element_type=F32)


def w_slot(w):
    return (w, 16) if w < PEERS else (FAR_TILES + w - PEERS, 0)


def pack_kernel(h_ref, c_ref, w_ref, out_ref):
    y = lax.broadcasted_iota(jnp.int32, (2 * OCC, 128), 0)
    col = lax.broadcasted_iota(jnp.int32, (2 * OCC, 128), 1)
    pick = (col == jnp.where(y < OCC, y, y + BANDS - OCC)).astype(F32).astype(BF)
    for ob in range(FAR_TILES // 2):
        far = lax.dot_general(
            pick,
            c_ref[ob * 128 : (ob + 1) * 128, :],
            (((1,), (1,)), ((), ())),
            preferred_element_type=F32,
        ).astype(BF)
        out_ref[2 * ob, 0:16, :] = far[0:16]
        out_ref[2 * ob + 1, 0:16, :] = far[16:32]
    row0 = h_ref[0] * HALF
    r16 = lax.broadcasted_iota(jnp.int32, (16, 128), 0)
    c16 = lax.broadcasted_iota(jnp.int32, (16, 128), 1)
    for rb in range(HALF // 16):
        for cb in range(NAUX // 128):
            above = (c16 + cb * 128) - (r16 + rb * 16) - row0
            rows = slice(rb * 16, rb * 16 + 16)
            wr = w_ref[rows, cb * 128 : cb * 128 + 128].astype(F32)
            wi = w_ref[rows, NAUX + cb * 128 : NAUX + cb * 128 + 128].astype(F32)
            packed = jnp.where(above > 0, wr, jnp.where(above == 0, 0.5 * wr, wi))
            j, at = w_slot(rb * (NAUX // 128) + cb)
            out_ref[j, at : at + 16, :] = packed.astype(BF)
    for j in range(FAR_TILES + W_TILES - PEERS, PEERS):
        out_ref[j, 0:16, :] = jnp.zeros((16, 128), BF)


def route_kernel(s_ref, partner_ref, r_ref, own_ref, got_ref, out_ref):
    first = s_ref[0] == 0
    is_far = s_ref[1] < FAR_TILES
    own, got = own_ref[0].astype(F32), got_ref[0].astype(F32)
    halves = (
        jnp.where(first, own, got).astype(BF),
        jnp.where(first, got, own).astype(BF),
    )
    for k in range(PEERS):
        out_ref[k, 16:32, :] = halves[k % 2][16:32]

    @pl.when(is_far)
    def _():
        for k in range(PEERS):
            out_ref[k, 0:16, :] = r_ref[partner_ref[k], 0:16, :]

    @pl.when(jnp.logical_not(is_far))
    def _():
        for k in range(PEERS):
            out_ref[k, 0:16, :] = halves[k % 2][0:16]


GROUP = 4
STEPS = ATOMS // GROUP


def pair_kernel(h_ref, nbr_ref, far_ref, own_ref, oth_ref, c_ref, out_ref, x_ref, w_ref, p_ref):
    step = pl.program_id(0)
    h = h_ref[0]
    low32 = lax.broadcasted_iota(jnp.int32, (2 * OCC, 128), 1) < ORBS

    @pl.when(step == 0)
    def _():
        for ob in range(FAR_TILES // 2):
            both = jnp.concatenate(
                [far_ref[2 * ob, 0:16, :], far_ref[2 * ob + 1, 0:16, :]], axis=0
            ).astype(F32)
            turned = pltpu.roll(both, 64, 1)
            x_ref[2 * ob] = jnp.where(low32, both, turned).astype(BF)
            x_ref[2 * ob + 1] = jnp.where(low32, turned, both).astype(BF)
        w_ref[...] = jnp.zeros_like(w_ref)

    def group(triple_ref, half):
        for g in range(GROUP):
            at = step * GROUP + g
            n0 = nbr_ref[at, 0]
            n1 = nbr_ref[at, 1]
            lhs = jnp.where(
                low32, x_ref[n0].astype(F32), x_ref[n1].astype(F32)
            ).astype(BF)
            pair = dot(lhs, triple_ref[g]).astype(BF)
            atom = half * (ATOMS // 2) + lax.rem(at, ATOMS // 2)
            own = c_ref[pl.ds(pl.multiple_of(atom * ORBS, ORBS), ORBS), :].astype(F32)
            sign = jnp.where(lax.broadcasted_iota(jnp.int32, own.shape, 1) < BANDS, 1.0, -1.0)
            first = (own * sign).astype(BF)
            second = pltpu.roll(own, BANDS, 1).astype(BF)
            w_ref[g, 0:64, 0:128] = first
            w_ref[g, 64:128, 128:256] = first
            w_ref[g, 128:192, 0:128] = second
            w_ref[g, 192:256, 128:256] = second
            left = jnp.concatenate(
                [
                    jnp.concatenate(
                        [pair[0:16, q * 128 : q * 128 + 128], pair[16:32, q * 128 : q * 128 + 128]],
                        axis=1,
                    )
                    for q in range(AUX_ATOM // 2)
                ],
                axis=0,
            )
            prod = dot(left, w_ref[g])
            for q in range(AUX_ATOM // 2):
                for e in range(2):
                    mu = atom * AUX_ATOM + 2 * q + e
                    for s in range(2):
                        p_ref[pl.ds(mu + s * 8 * NAUX, 8, stride=NAUX), :] = prod[
                            q * 16 + s * 8 : q * 16 + s * 8 + 8, e * 128 : e * 128 + 128
                        ]

    @pl.when(step < STEPS // 2)
    def _():
        group(own_ref, h)

    @pl.when(step >= STEPS // 2)
    def _():
        group(oth_ref, 1 - h)

    @pl.when(step == STEPS - 1)
    def _():
        for l in range(OCC):
            out_ref[l] = p_ref[l * NAUX : (l + 1) * NAUX, :].astype(BF)


BLK = 256
NB = NAUX // BLK


def sigma_kernel(s_ref, p_ref, wa_ref, wb_ref, keep_ref, send_ref, a_ref, b_ref, acc_ref, sig_ref):
    pair = pl.program_id(0)

    @pl.when(pair == 0)
    def _():
        core0 = s_ref[1] == 0
        r16 = lax.broadcasted_iota(jnp.int32, (16, 128), 0)
        c16 = lax.broadcasted_iota(jnp.int32, (16, 128), 1)
        for half in range(2):
            for rb in range(HALF // 16):
                row = half * HALF + rb * 16
                blk, at = row // BLK, row % BLK
                for cb in range(NAUX // 128):
                    j, base = w_slot(rb * (NAUX // 128) + cb)
                    va = wa_ref[j, base : base + 16, :].astype(F32)
                    vb = wb_ref[j, base : base + 16, :].astype(F32)
                    tile = jnp.where(core0, va, vb) if half == 0 else jnp.where(core0, vb, va)
                    cblk, cat = cb * 128 // BLK, cb * 128 % BLK
                    above = (c16 + cb * 128) - (r16 + row)
                    if cblk >= blk:
                        lo = (cblk - blk) * BLK + cat
                        up = tile if cblk > blk else jnp.where(above >= 0, tile, 0.0)
                        a_ref[blk, at : at + 16, lo : lo + 128] = up.astype(BF)
                    if cblk <= blk:
                        lo = (NB - blk + cblk) * BLK + cat
                        down = tile if cblk < blk else jnp.where(above < 0, tile, 0.0)
                        a_ref[blk, at : at + 16, lo : lo + 128] = down.astype(BF)
        acc_ref[...] = jnp.zeros_like(acc_ref)

    low = lax.broadcasted_iota(jnp.int32, (NAUX, 128), 1) < BANDS
    for s in range(2):
        val = p_ref[s]
        b_ref[0:NAUX, s * 128 : s * 128 + 128] = val
        turned = pltpu.roll(val.astype(F32), BANDS, 1)
        b_ref[NAUX : 2 * NAUX, s * 128 : s * 128 + 128] = jnp.where(low, -turned, turned).astype(BF)
    for blk in range(NB):
        scr = dot(a_ref[blk], b_ref[blk * BLK : blk * BLK + (NB + 1) * BLK, :]).astype(BF)
        for s in range(2):
            acc_ref[...] += lax.dot_general(
                p_ref[s, blk * BLK : blk * BLK + BLK, :],
                scr[:, s * 128 : s * 128 + 128],
                (((0,), (0,)), ((), ())),
                preferred_element_type=F32,
            )

    @pl.when(pair == pl.num_programs(0) - 1)
    def _():
        y = acc_ref[...]
        z = y + y.T
        re = z[:BANDS, :BANDS] + z[BANDS:, BANDS:]
        im = z[:BANDS, BANDS:] - z[BANDS:, :BANDS]
        sig_ref[...] = PREFACTOR * jnp.concatenate([re, im], axis=1)
        h = s_ref[0]
        rows = BANDS // 2
        keep_ref[...] = sig_ref[pl.ds(pl.multiple_of(h * rows, rows), rows), :]
        send_ref[...] = sig_ref[pl.ds(pl.multiple_of((1 - h) * rows, rows), rows), :]


def params():
    return pltpu.CompilerParams(vmem_limit_bytes=VMEM)


def whole(shape):
    return pl.BlockSpec(shape, lambda i, *_: (0,) * len(shape))


def local(coefficients, triple, neighbors, w_screened, partner, q_ids):
    h = lax.axis_index("aux").astype(jnp.int32)
    me = lax.axis_index(KA).astype(jnp.int32)
    core = lax.axis_index("core").astype(jnp.int32)
    swap = [(0, 1), (1, 0)]
    atoms = triple.shape[0]
    coef = coefficients[0]
    triple = triple.reshape(atoms, 2 * ORBS, AUX_ATOM * ORBS)

    share = atoms // 8
    mine = lax.axis_index(("y", "core")) * share
    crossed = lax.ppermute(lax.dynamic_slice_in_dim(triple, mine, share, 0), "aux", swap)
    nbr_other = lax.ppermute(neighbors, "aux", swap)
    nbr = jnp.concatenate([neighbors, nbr_other], axis=0)

    smem = pl.BlockSpec(memory_space=pltpu.SMEM)
    vmem = pl.BlockSpec(memory_space=pltpu.VMEM)
    piece = jax.ShapeDtypeStruct((PEERS, 32, 128), BF)
    packed = pl.pallas_call(
        pack_kernel,
        out_shape=piece,
        in_specs=[smem, vmem, vmem],
        out_specs=vmem,
        compiler_params=params(),
        name="pack",
    )(h[None], coef, w_screened[0])
    spread = lax.all_to_all(packed, KA, split_axis=0, concat_axis=0, tiled=True)

    crossed, spread = lax.optimization_barrier((crossed, spread))
    other = lax.all_gather(crossed, ("y", "core"), axis=0, tiled=True)

    own_tile = lax.dynamic_slice_in_dim(spread, q_ids[h], 1, 0)
    got_tile = lax.ppermute(
        lax.dynamic_slice_in_dim(spread, q_ids[1 - h], 1, 0), "aux", swap
    )
    partner_here = lax.dynamic_slice_in_dim(partner, h, 1, 0)[0]
    routed = pl.pallas_call(
        route_kernel,
        out_shape=piece,
        in_specs=[smem, smem, vmem, vmem, vmem],
        out_specs=vmem,
        compiler_params=params(),
        name="route",
    )(jnp.stack([h, me]), partner_here, spread, own_tile, got_tile)
    arrived = lax.all_to_all(routed, KA, split_axis=0, concat_axis=0, tiled=True)
    arrived2 = lax.ppermute(arrived, "core", swap)

    half_steps = STEPS // 2
    products = pl.pallas_call(
        pair_kernel,
        out_shape=jax.ShapeDtypeStruct((OCC, NAUX, 128), BF),
        grid=(STEPS,),
        in_specs=[
            smem,
            smem,
            whole((PEERS, 32, 128)),
            pl.BlockSpec(
                (GROUP, 2 * ORBS, AUX_ATOM * ORBS),
                lambda i: (jnp.minimum(i, half_steps - 1), 0, 0),
            ),
            pl.BlockSpec(
                (GROUP, 2 * ORBS, AUX_ATOM * ORBS),
                lambda i: (jnp.maximum(i - half_steps, 0), 0, 0),
            ),
            whole((ATOMS * ORBS, 128)),
        ],
        out_specs=whole((OCC, NAUX, 128)),
        scratch_shapes=[
            pltpu.VMEM((ATOMS, 2 * OCC, 128), BF),
            pltpu.VMEM((GROUP, 256, 256), BF),
            pltpu.VMEM((OCC * NAUX, 128), F32),
        ],
        compiler_params=params(),
        cost_estimate=pl.CostEstimate(flops=4_000_000_000, bytes_accessed=17_000_000, transcendentals=0),
        name="pair_products",
    )(h[None], nbr, arrived, triple, other, coef)

    rows = BANDS // 2
    part = jax.ShapeDtypeStruct((rows, 2 * BANDS), F32)
    keep, send = pl.pallas_call(
        sigma_kernel,
        out_shape=(part, part),
        grid=(OCC // 2,),
        in_specs=[
            smem,
            pl.BlockSpec((2, NAUX, 128), lambda i: (i, 0, 0)),
            whole((PEERS, 32, 128)),
            whole((PEERS, 32, 128)),
        ],
        out_specs=(whole((rows, 2 * BANDS)),) * 2,
        scratch_shapes=[
            pltpu.VMEM((NB, BLK, (NB + 1) * BLK), BF),
            pltpu.VMEM((2 * NAUX, 256), BF),
            pltpu.VMEM((128, 128), F32),
            pltpu.VMEM((BANDS, 128), F32),
        ],
        compiler_params=params(),
        name="screened_sigma",
    )(jnp.stack([h, core]), products, arrived, arrived2)
    return (keep + lax.ppermute(send, "aux", swap))[None]


def solution(mesh):
    ka, aux = mesh.devices.shape
    fine = Mesh(mesh.devices.reshape(8, 2, 4, 2, aux), (*KA, "aux"))
    in_specs = (
        P(KA, None, None),
        P("aux", None, None, None),
        P("aux", None),
        P(KA, "aux", None),
        P(),
        P(),
    )
    return jax.shard_map(
        local, mesh=fine, in_specs=in_specs, out_specs=P(KA, "aux", None), check_vma=False
    )
```

```python
import functools
import math

import jax
import jax.numpy as jnp
import numpy as np
from jax import lax
from jax.experimental import pallas as pl
from jax.experimental.pallas import tpu as pltpu
from jax.sharding import Mesh
from jax.sharding import PartitionSpec as P

ATOMS = 64
ORBS = 64
AUX_ATOM = 12
BANDS = 64
OCC = 16
TRANSFERS = 2
NAUX = ATOMS * AUX_ATOM
HALF = NAUX // 2
BF = jnp.bfloat16
F32 = jnp.float32
KA = ("z", "xl", "y", "core")
BY_CORE = ("core", "z", "xl", "y")
PEERS = 128
FAR = 2 * OCC * ATOMS * ORBS // 128
FAR_ROWS = FAR // PEERS
PACKED = HALF * NAUX // 128
W_ROWS = PACKED // PEERS
PIECE = FAR_ROWS + W_ROWS
PREFACTOR = -1.0 / math.sqrt(TRANSFERS * NAUX * OCC)


def dot(a, b):
    return jnp.dot(a, b, preferred_element_type=F32)


def w_tile(row, lane):
    at = (row // 16 * (NAUX // 128) + lane // 128) * 16
    return slice(at, at + 16)


def pack_kernel(s_ref, c_ref, w_ref, triple_ref, out_ref, share_ref, stage_ref, in_sem, out_sem):
    parts = in_sem.shape[0]
    size = share_ref.shape[0] // parts
    reads, writes = [], []
    for n in range(parts):
        rows = pl.ds(n * size, size)
        reads.append(
            pltpu.make_async_copy(
                triple_ref.at[pl.ds(s_ref[1] * share_ref.shape[0] + n * size, size)],
                stage_ref.at[rows],
                in_sem.at[n],
            )
        )
        writes.append(pltpu.make_async_copy(stage_ref.at[rows], share_ref.at[rows], out_sem.at[n]))
    for copy in reads:
        copy.start()
    y = lax.broadcasted_iota(jnp.int32, (2 * OCC, 128), 0)
    col = lax.broadcasted_iota(jnp.int32, (2 * OCC, 128), 1)
    pick = (col == jnp.where(y < OCC, y, y + BANDS - OCC)).astype(F32).astype(BF)
    for ob in range(ATOMS // 2):
        far = lax.dot_general(
            pick,
            c_ref[ob * 128 : (ob + 1) * 128, :],
            (((1,), (1,)), ((), ())),
            preferred_element_type=F32,
        )
        for i in range(4):
            at = (4 * ob + i) * PIECE
            out_ref[at : at + FAR_ROWS, :] = far[i * 8 : i * 8 + 8].astype(BF)
    for read, write in zip(reads, writes):
        read.wait()
        write.start()
    row0 = s_ref[0] * HALF
    r16 = lax.broadcasted_iota(jnp.int32, (16, 128), 0)
    c16 = lax.broadcasted_iota(jnp.int32, (16, 128), 1)
    for row in range(0, HALF, 16):
        for lane in range(0, NAUX, 128):
            above = (c16 + lane) - (r16 + row) - row0
            rows = slice(row, row + 16)
            wr = w_ref[rows, lane : lane + 128].astype(F32)
            wi = w_ref[rows, NAUX + lane : NAUX + lane + 128].astype(F32)
            packed = jnp.where(above > 0, wr, jnp.where(above == 0, 0.5 * wr, wi))
            packed = packed.astype(BF)
            tile = w_tile(row, lane)
            a = tile.start
            while a < tile.stop:
                piece, at = divmod(a, W_ROWS)
                b = min(tile.stop, a - at + W_ROWS)
                to = piece * PIECE + FAR_ROWS + at
                out_ref[to : to + b - a, :] = packed[a - tile.start : b - tile.start]
                a = b
    for write in writes:
        write.wait()


def route_kernel(h_ref, partner_ref, r_ref, own_ref, got_ref, out_ref):
    split = FAR_ROWS // 2
    first = h_ref[0] == 0

    def fill(halves):
        for k in range(PEERS):
            out_ref[k, split:] = halves[k // (PEERS // 2)][0]

    pl.when(first)(lambda: fill((own_ref, got_ref)))
    pl.when(jnp.logical_not(first))(lambda: fill((got_ref, own_ref)))
    for k in range(PEERS):
        out_ref[k, 0:split] = r_ref[partner_ref[k], 0:split]


OWN_MIB = 48
GROUP = 8
GROUP_AUX = GROUP * AUX_ATOM
PITCH = GROUP_AUX + 1


def spread_far(far_ref, x_ref):
    low32 = lax.broadcasted_iota(jnp.int32, (2 * OCC, 128), 1) < ORBS
    for ob in range(ATOMS // 2):
        tops = [(4 * ob + i) * PIECE for i in range(4)]
        both = jnp.concatenate([far_ref[a : a + FAR_ROWS, :].astype(F32) for a in tops], axis=0)
        turned = pltpu.roll(both, 64, 1)
        x_ref[2 * ob] = jnp.where(low32, both, turned).astype(BF)
        x_ref[2 * ob + 1] = jnp.where(low32, turned, both).astype(BF)


def pair_kernel(s_ref, nbr_ref, far_ref, x_ref, triple_ref, coef_ref, out_ref, stage_ref, c_ref, w_ref, p_ref, sems):
    step = pl.program_id(0)
    low32 = lax.broadcasted_iota(jnp.int32, (2 * OCC, 128), 1) < ORBS

    def fetch(n):
        rows = pl.ds(n * GROUP, GROUP)
        return pltpu.make_async_copy(triple_ref.at[rows], stage_ref.at[rows], sems.at[n])

    def fetch_own():
        rows = pl.ds(pl.multiple_of(s_ref[0] * ORBS, ORBS), c_ref.shape[0])
        return pltpu.make_async_copy(coef_ref.at[rows], c_ref, sems.at[sems.shape[0] - 1])

    @pl.when(step == 0)
    def _():
        fetch(0).start()
        fetch_own().start()
        for n in range(1, stage_ref.shape[0] // GROUP):
            fetch(n).start()
        w_ref[...] = jnp.zeros_like(w_ref)
        if far_ref is not None:
            spread_far(far_ref, x_ref)
        fetch_own().wait()

    fetch(step).wait()
    for g in range(GROUP):
        at = step * GROUP + g
        n0 = nbr_ref[s_ref[1] + at, 0]
        n1 = nbr_ref[s_ref[1] + at, 1]
        lhs = jnp.where(low32, x_ref[n0].astype(F32), x_ref[n1].astype(F32)).astype(BF)
        pair = dot(lhs, stage_ref[at]).astype(BF)
        own = c_ref[pl.ds(pl.multiple_of(at * ORBS, ORBS), ORBS), :].astype(F32)
        sign = jnp.where(lax.broadcasted_iota(jnp.int32, own.shape, 1) < BANDS, 1.0, -1.0)
        first = (own * sign).astype(BF)
        second = pltpu.roll(own, BANDS, 1).astype(BF)
        w_ref[g, 0:64, 0:128] = first
        w_ref[g, 64:128, 128:256] = first
        w_ref[g, 128:192, 0:128] = second
        w_ref[g, 192:256, 128:256] = second
        left = jnp.concatenate(
            [
                jnp.concatenate(
                    [pair[0:16, q * 128 : q * 128 + 128], pair[16:32, q * 128 : q * 128 + 128]],
                    axis=1,
                )
                for q in range(AUX_ATOM // 2)
            ],
            axis=0,
        )
        prod = dot(left, w_ref[g])
        for q in range(AUX_ATOM // 2):
            for e in range(2):
                mu = g * AUX_ATOM + 2 * q + e
                for s in range(2):
                    p_ref[pl.ds(mu + s * 8 * PITCH, 8, stride=PITCH), :] = prod[
                        q * 16 + s * 8 : q * 16 + s * 8 + 8, e * 128 : e * 128 + 128
                    ]

    rows = pl.ds(pl.multiple_of(step * GROUP_AUX, GROUP_AUX), GROUP_AUX)
    for l in range(OCC):
        out_ref[l, rows, :] = p_ref[l * PITCH : l * PITCH + GROUP_AUX, :].astype(BF)


def pair_products(first, row, nbr, x, triple, coef, into=None, mib=24):
    count = triple.shape[0]
    extra = () if into is None else (into,)

    def kernel(s_ref, nbr_ref, x_ref, triple_ref, c_ref, *rest):
        if extra:
            pair_kernel(s_ref, nbr_ref, None, x_ref, triple_ref, c_ref, *rest[len(extra) :])
        else:
            out_ref, made_ref, *scratch = rest
            pair_kernel(s_ref, nbr_ref, x_ref, made_ref, triple_ref, c_ref, out_ref, *scratch)

    vmem = pl.BlockSpec(memory_space=pltpu.VMEM)
    out_shape = jax.ShapeDtypeStruct((OCC, NAUX, 128), BF)
    out_spec = pl.BlockSpec((OCC, count * AUX_ATOM, 128), lambda i, s, _: (0, s[0] // count, 0))
    made = jax.ShapeDtypeStruct((ATOMS, 2 * OCC, 128), BF)
    return pl.pallas_call(
        kernel,
        out_shape=out_shape if extra else (out_shape, made),
        grid_spec=pltpu.PrefetchScalarGridSpec(
            num_scalar_prefetch=2,
            grid=(count // GROUP,),
            in_specs=[
                whole(made.shape) if extra else vmem,
                pl.BlockSpec(memory_space=pltpu.HBM),
                pl.BlockSpec(memory_space=pltpu.HBM),
                *(pl.BlockSpec(memory_space=pl.ANY) for _ in extra),
            ],
            out_specs=out_spec if extra else (out_spec, whole(made.shape)),
            scratch_shapes=[
                pltpu.VMEM(triple.shape, BF),
                pltpu.VMEM((count * ORBS, 128), BF),
                pltpu.VMEM((GROUP, 256, 256), BF),
                pltpu.VMEM((OCC * PITCH + 8, 128), F32),
                pltpu.SemaphoreType.DMA((count // GROUP + 1,)),
            ],
        ),
        input_output_aliases={5: 0} if extra else {},
        compiler_params=params(mib),
        cost_estimate=pl.CostEstimate(
            flops=count * 200_000_000, bytes_accessed=count * 250_000, transcendentals=0
        ),
        name="pair_products",
    )(jnp.stack([first, row]), nbr, x, triple, coef, *extra)


BLK = 256
NB = NAUX // BLK
BATCH = 4


def sigma_kernel(s_ref, p_ref, wa_ref, wb_ref, keep_ref, send_ref, re_ref, im_ref, acc_ref, sig_ref):
    step = pl.program_id(0)

    @pl.when(step == 0)
    def _():
        core0 = s_ref[1] == 0
        r16 = lax.broadcasted_iota(jnp.int32, (16, 128), 0)
        c16 = lax.broadcasted_iota(jnp.int32, (16, 128), 1)
        for half in range(2):
            for row in range(0, HALF, 16):
                for lane in range(0, NAUX, 128):
                    here = wa_ref[w_tile(row, lane), :].astype(F32)
                    there = wb_ref[w_tile(row, lane), :].astype(F32)
                    tile = jnp.where(core0, there, here) if half else jnp.where(core0, here, there)
                    mu = half * HALF + row
                    above = (c16 + lane) - (r16 + mu)
                    at = (slice(mu, mu + 16), slice(lane, lane + 128))
                    if lane // BLK >= mu // BLK:
                        re_ref[at] = jnp.where(above >= 0, tile, 0.0).astype(BF)
                    if lane // BLK <= mu // BLK:
                        im_ref[at] = jnp.where(above < 0, tile, 0.0).astype(BF)
        acc_ref[...] = jnp.zeros_like(acc_ref)

    p = [p_ref[s] for s in range(BATCH)]
    wide = jnp.concatenate(p, axis=1)
    acc = acc_ref[...]
    for blk in range(NB):
        a, b = blk * BLK, blk * BLK + BLK
        re = dot(re_ref[a:b, a:NAUX], wide[a:NAUX]).astype(BF)
        im = dot(im_ref[a:b, 0:b], wide[0:b]).astype(BF)
        for s in range(BATCH):
            lanes = slice(s * 128, s * 128 + 128)
            acc += lax.dot_general(
                p[s][a:b],
                jnp.concatenate([re[:, lanes], im[:, lanes]], axis=1),
                (((0,), (0,)), ((), ())),
                preferred_element_type=F32,
            )
    acc_ref[...] = acc

    @pl.when(step == pl.num_programs(0) - 1)
    def _():
        yi = acc_ref[:, 128:256]
        low = lax.broadcasted_iota(jnp.int32, yi.shape, 1) < BANDS
        turned = pltpu.roll(yi, BANDS, 1)
        y = acc_ref[:, 0:128] + jnp.where(low, -turned, turned)
        z = y + y.T
        re = z[:BANDS, :BANDS] + z[BANDS:, BANDS:]
        im = z[:BANDS, BANDS:] - z[BANDS:, :BANDS]
        sig_ref[...] = PREFACTOR * jnp.concatenate([re, im], axis=1)
        h = s_ref[0]
        rows = BANDS // 2
        keep_ref[...] = sig_ref[pl.ds(pl.multiple_of(h * rows, rows), rows), :]
        send_ref[...] = sig_ref[pl.ds(pl.multiple_of((1 - h) * rows, rows), rows), :]


def screened_sigma(h, core, products, here, there):
    rows = BANDS // 2
    part = jax.ShapeDtypeStruct((rows, 2 * BANDS), F32)
    return pl.pallas_call(
        sigma_kernel,
        out_shape=(part, part),
        grid=(OCC // BATCH,),
        in_specs=[
            pl.BlockSpec(memory_space=pltpu.SMEM),
            pl.BlockSpec((BATCH, NAUX, 128), lambda i: (i, 0, 0)),
            pl.BlockSpec(memory_space=pltpu.VMEM),
            pl.BlockSpec(memory_space=pltpu.VMEM),
        ],
        out_specs=(whole((rows, 2 * BANDS)),) * 2,
        scratch_shapes=[
            pltpu.VMEM((NAUX, NAUX), BF),
            pltpu.VMEM((NAUX, NAUX), BF),
            pltpu.VMEM((128, 256), F32),
            pltpu.VMEM((BANDS, 128), F32),
        ],
        compiler_params=params(24),
        name="screened_sigma",
    )(jnp.stack([h, core]), products, here, there)


def place(k):
    return k % 2 * (PEERS // 2) + k // 2


def by_core(ids):
    return place(ids).reshape(PEERS // 2, 2).T.reshape(PEERS)


def params(mib):
    return pltpu.CompilerParams(vmem_limit_bytes=mib * 2**20)


def whole(shape):
    return pl.BlockSpec(shape, lambda i, *_: (0,) * len(shape))


def x_crossing():
    ids = np.arange(8 * 2 * 4 * 2 * 2).reshape(8, 2, 4, 2, 2)
    pairs = []
    for z, xl, y, core, aux in np.ndindex(ids.shape):
        pairs.append((int(ids[z, xl, y, core, aux]), int(ids[z, 1 - xl, y, core, 1 - aux])))
    return pairs


def local(coefficients, triple, neighbors, w_screened, partner, q_ids):
    h = lax.axis_index("aux").astype(jnp.int32)
    me = lax.axis_index(KA).astype(jnp.int32)
    core = lax.axis_index("core").astype(jnp.int32)
    swap = [(0, 1), (1, 0)]
    atoms = triple.shape[0]
    coef = coefficients[0]
    triple = triple.reshape(atoms, 2 * ORBS, AUX_ATOM * ORBS)

    share = atoms // 2
    nbr_other = lax.ppermute(neighbors, "aux", swap)

    smem = pl.BlockSpec(memory_space=pltpu.SMEM)
    vmem = pl.BlockSpec(memory_space=pltpu.VMEM)
    hbm = pl.BlockSpec(memory_space=pl.ANY)
    shared = (share, *triple.shape[1:])
    pieces, sent = pl.pallas_call(
        pack_kernel,
        out_shape=(
            jax.ShapeDtypeStruct((PEERS * PIECE, 128), BF),
            jax.ShapeDtypeStruct(shared, BF),
        ),
        in_specs=[smem, vmem, vmem, hbm],
        out_specs=(vmem, hbm),
        scratch_shapes=[
            pltpu.VMEM(shared, BF),
            pltpu.SemaphoreType.DMA((4,)),
            pltpu.SemaphoreType.DMA((4,)),
        ],
        compiler_params=params(56),
        name="pack",
    )(jnp.stack([h, core]), coef, w_screened[0], triple)
    crossed = lax.ppermute(sent, (*KA, "aux"), x_crossing())

    spread = lax.all_to_all(
        pieces.reshape(PEERS, PIECE // 2, 2, 128), BY_CORE, split_axis=0, concat_axis=0, tiled=True
    )
    partner_here = by_core(lax.dynamic_slice_in_dim(partner, h, 1, 0)[0])
    partner_here, q_place, nbr_other = lax.optimization_barrier(
        (partner_here, place(q_ids), nbr_other)
    )
    split = FAR_ROWS // 2

    def own_piece(t):
        return lax.dynamic_slice(spread, (q_place[t], split, 0, 0), (1, W_ROWS // 2, 2, 128))

    got = lax.ppermute(own_piece(1 - h), "aux", swap)
    routed = pl.pallas_call(
        route_kernel,
        out_shape=jax.ShapeDtypeStruct(spread.shape, BF),
        in_specs=[smem, smem, vmem, vmem, vmem],
        out_specs=vmem,
        compiler_params=params(12),
        name="route",
    )(h[None], partner_here, spread, own_piece(h), got)
    arrived = lax.all_to_all(routed, BY_CORE, split_axis=0, concat_axis=0, tiled=True)

    crossed, arrived = lax.optimization_barrier((crossed, arrived))
    crossed2 = lax.ppermute(crossed, "core", swap)
    here = arrived[:, split:].reshape(PACKED, 128)
    there = lax.ppermute(here, "core", swap)
    far = arrived.reshape(PEERS * PIECE, 128)
    zero = jnp.zeros_like(h)
    others = (1 - h) * atoms
    products, x = pair_products(h * atoms, zero, neighbors, far, triple, coef, mib=OWN_MIB)
    near, away = core * share, (1 - core) * share
    products = pair_products(others + near, near, nbr_other, x, crossed, coef, products)
    products = pair_products(others + away, away, nbr_other, x, crossed2, coef, products)
    keep, send = screened_sigma(h, core, products, here, there)
    return (keep + lax.ppermute(send, "aux", swap))[None]


def solution(mesh):
    ka, aux = mesh.devices.shape
    fine = Mesh(mesh.devices.reshape(8, 2, 4, 2, aux), (*KA, "aux"))
    in_specs = (
        P(KA, None, None),
        P("aux", None, None, None),
        P("aux", None),
        P(KA, "aux", None),
        P(),
        P(),
    )
    return jax.shard_map(
        local, mesh=fine, in_specs=in_specs, out_specs=P(KA, "aux", None), check_vma=False
    )
```

```python
import functools
import math

import jax
import jax.numpy as jnp
import numpy as np
from jax import lax
from jax.experimental import pallas as pl
from jax.experimental.pallas import tpu as pltpu
from jax.sharding import Mesh
from jax.sharding import PartitionSpec as P

ATOMS = 64
ORBS = 64
AUX_ATOM = 12
BANDS = 64
OCC = 16
TRANSFERS = 2
NAUX = ATOMS * AUX_ATOM
HALF = NAUX // 2
BF = jnp.bfloat16
F32 = jnp.float32
KA = ("z", "xl", "y", "core")
BY_CORE = ("core", "z", "xl", "y")
PEERS = 128
FAR = 2 * OCC * ATOMS * ORBS // 128
FAR_ROWS = FAR // PEERS
PACKED = HALF * NAUX // 128
W_ROWS = PACKED // PEERS
PIECE = FAR_ROWS + W_ROWS
PREFACTOR = -1.0 / math.sqrt(TRANSFERS * NAUX * OCC)


def dot(a, b):
    return jnp.dot(a, b, preferred_element_type=F32)


def w_tile(row, lane):
    at = (row // 16 * (NAUX // 128) + lane // 128) * 16
    return slice(at, at + 16)


def pack_kernel(h_ref, c_ref, w_ref, out_ref):
    y = lax.broadcasted_iota(jnp.int32, (2 * OCC, 128), 0)
    col = lax.broadcasted_iota(jnp.int32, (2 * OCC, 128), 1)
    pick = (col == jnp.where(y < OCC, y, y + BANDS - OCC)).astype(F32).astype(BF)
    for ob in range(ATOMS // 2):
        far = lax.dot_general(
            pick,
            c_ref[ob * 128 : (ob + 1) * 128, :],
            (((1,), (1,)), ((), ())),
            preferred_element_type=F32,
        )
        for i in range(4):
            at = (4 * ob + i) * PIECE
            out_ref[at : at + FAR_ROWS, :] = far[i * 8 : i * 8 + 8].astype(BF)
    row0 = h_ref[0] * HALF
    r16 = lax.broadcasted_iota(jnp.int32, (16, 128), 0)
    c16 = lax.broadcasted_iota(jnp.int32, (16, 128), 1)
    for row in range(0, HALF, 16):
        for lane in range(0, NAUX, 128):
            above = (c16 + lane) - (r16 + row) - row0
            rows = slice(row, row + 16)
            wr = w_ref[rows, lane : lane + 128].astype(F32)
            wi = w_ref[rows, NAUX + lane : NAUX + lane + 128].astype(F32)
            packed = jnp.where(above > 0, wr, jnp.where(above == 0, 0.5 * wr, wi))
            packed = packed.astype(BF)
            tile = w_tile(row, lane)
            a = tile.start
            while a < tile.stop:
                piece, at = divmod(a, W_ROWS)
                b = min(tile.stop, a - at + W_ROWS)
                to = piece * PIECE + FAR_ROWS + at
                out_ref[to : to + b - a, :] = packed[a - tile.start : b - tile.start]
                a = b


def route_kernel(h_ref, partner_ref, r_ref, own_ref, got_ref, out_ref):
    split = FAR_ROWS // 2
    first = h_ref[0] == 0

    def fill(halves):
        for k in range(PEERS):
            out_ref[k, split:] = halves[k // (PEERS // 2)][0]

    pl.when(first)(lambda: fill((own_ref, got_ref)))
    pl.when(jnp.logical_not(first))(lambda: fill((got_ref, own_ref)))
    for k in range(PEERS):
        out_ref[k, 0:split] = r_ref[partner_ref[k], 0:split]


OWN_MIB = 48
GROUP = 8
GROUP_AUX = GROUP * AUX_ATOM
PITCH = GROUP_AUX + 1


def spread_far(far_ref, x_ref):
    low32 = lax.broadcasted_iota(jnp.int32, (2 * OCC, 128), 1) < ORBS
    for ob in range(ATOMS // 2):
        tops = [(4 * ob + i) * FAR_ROWS for i in range(4)]
        both = jnp.concatenate([far_ref[a : a + FAR_ROWS, :].astype(F32) for a in tops], axis=0)
        turned = pltpu.roll(both, 64, 1)
        x_ref[2 * ob] = jnp.where(low32, both, turned).astype(BF)
        x_ref[2 * ob + 1] = jnp.where(low32, turned, both).astype(BF)


def pair_kernel(s_ref, nbr_ref, far_ref, x_ref, triple_refs, coef_ref, out_ref, stage_ref, c_ref, w_ref, p_ref, sems):
    step = pl.program_id(0)
    low32 = lax.broadcasted_iota(jnp.int32, (2 * OCC, 128), 1) < ORBS

    count = stage_ref.shape[0]
    steps = count // GROUP
    each = steps // len(triple_refs)

    def fetch(n):
        source = triple_refs[n // each].at[pl.ds(n % each * GROUP, GROUP)]
        return pltpu.make_async_copy(source, stage_ref.at[pl.ds(n * GROUP, GROUP)], sems.at[n])

    def fetch_own():
        rows = pl.ds(pl.multiple_of(s_ref[0] * ORBS, ORBS), c_ref.shape[0])
        return pltpu.make_async_copy(coef_ref.at[rows], c_ref, sems.at[sems.shape[0] - 1])

    @pl.when(step == 0)
    def _():
        fetch(0).start()
        fetch_own().start()
        for n in range(1, steps):
            fetch(n).start()
        w_ref[...] = jnp.zeros_like(w_ref)
        if far_ref is not None:
            spread_far(far_ref, x_ref)
        fetch_own().wait()

    for n in range(steps):
        pl.when(step == n)(fetch(n).wait)
    first_at = step * GROUP
    for g in range(GROUP):
        at = first_at + g
        n0 = nbr_ref[at, 0]
        n1 = nbr_ref[at, 1]
        lhs = jnp.where(low32, x_ref[n0].astype(F32), x_ref[n1].astype(F32)).astype(BF)
        pair = dot(lhs, stage_ref[step * GROUP + g]).astype(BF)
        own = c_ref[pl.ds(pl.multiple_of(at * ORBS, ORBS), ORBS), :].astype(F32)
        sign = jnp.where(lax.broadcasted_iota(jnp.int32, own.shape, 1) < BANDS, 1.0, -1.0)
        first = (own * sign).astype(BF)
        second = pltpu.roll(own, BANDS, 1).astype(BF)
        w_ref[g, 0:64, 0:128] = first
        w_ref[g, 64:128, 128:256] = first
        w_ref[g, 128:192, 0:128] = second
        w_ref[g, 192:256, 128:256] = second
        left = jnp.concatenate(
            [
                jnp.concatenate(
                    [pair[0:16, q * 128 : q * 128 + 128], pair[16:32, q * 128 : q * 128 + 128]],
                    axis=1,
                )
                for q in range(AUX_ATOM // 2)
            ],
            axis=0,
        )
        prod = dot(left, w_ref[g])
        for q in range(AUX_ATOM // 2):
            for e in range(2):
                mu = g * AUX_ATOM + 2 * q + e
                for s in range(2):
                    p_ref[pl.ds(mu + s * 8 * PITCH, 8, stride=PITCH), :] = prod[
                        q * 16 + s * 8 : q * 16 + s * 8 + 8, e * 128 : e * 128 + 128
                    ]

    rows = pl.ds(pl.multiple_of(first_at * AUX_ATOM, GROUP_AUX), GROUP_AUX)
    for l in range(OCC):
        out_ref[l, rows, :] = p_ref[l * PITCH : l * PITCH + GROUP_AUX, :].astype(BF)


def pair_products(first, nbr, x, triples, coef, into=None, after=None, mib=24):
    count = sum(t.shape[0] for t in triples)
    m = len(triples)
    extra = () if into is None else (into, after)

    def kernel(s_ref, nbr_ref, x_ref, *rest):
        triple_refs, coef_ref, rest = rest[:m], rest[m], rest[m + 1 :]
        if extra:
            pair_kernel(s_ref, nbr_ref, None, x_ref, triple_refs, coef_ref, *rest[2:])
        else:
            out_ref, made_ref, done_ref, *scratch = rest
            done_ref[...] = jnp.zeros_like(done_ref)
            pair_kernel(s_ref, nbr_ref, x_ref, made_ref, triple_refs, coef_ref, out_ref, *scratch)

    vmem = pl.BlockSpec(memory_space=pltpu.VMEM)
    out_shape = jax.ShapeDtypeStruct((OCC, NAUX, 128), BF)
    out_spec = pl.BlockSpec((OCC, count * AUX_ATOM, 128), lambda i, s, _: (0, s[0] // count, 0))
    made = jax.ShapeDtypeStruct((ATOMS, 2 * OCC, 128), BF)
    token = jax.ShapeDtypeStruct((8, 128), F32)
    return pl.pallas_call(
        kernel,
        out_shape=out_shape if extra else (out_shape, made, token),
        grid_spec=pltpu.PrefetchScalarGridSpec(
            num_scalar_prefetch=2,
            grid=(count // GROUP,),
            in_specs=[
                whole(made.shape) if extra else vmem,
                *(pl.BlockSpec(memory_space=pltpu.HBM) for _ in (*triples, coef)),
                *(pl.BlockSpec(memory_space=pl.ANY) for _ in extra),
            ],
            out_specs=out_spec if extra else (out_spec, whole(made.shape), whole(token.shape)),
            scratch_shapes=[
                pltpu.VMEM((count, *triples[0].shape[1:]), BF),
                pltpu.VMEM((count * ORBS, 128), BF),
                pltpu.VMEM((GROUP, 256, 256), BF),
                pltpu.VMEM((OCC * PITCH + 8, 128), F32),
                pltpu.SemaphoreType.DMA((count // GROUP + 1,)),
            ],
        ),
        input_output_aliases={m + 4: 0} if extra else {},
        compiler_params=params(mib),
        cost_estimate=pl.CostEstimate(
            flops=count * 200_000_000, bytes_accessed=count * 250_000, transcendentals=0
        ),
        name="pair_products",
    )(first[None], nbr, x, *triples, coef, *extra)


BLK = 256
NB = NAUX // BLK
BATCH = 8


def sigma_kernel(s_ref, p_ref, wa_ref, wb_ref, keep_ref, send_ref, re_ref, im_ref, acc_ref, sig_ref):
    step = pl.program_id(0)

    @pl.when(step == 0)
    def _():
        core0 = s_ref[1] == 0
        r16 = lax.broadcasted_iota(jnp.int32, (16, 128), 0)
        c16 = lax.broadcasted_iota(jnp.int32, (16, 128), 1)
        for half in range(2):
            for row in range(0, HALF, 16):
                for lane in range(0, NAUX, 128):
                    here = wa_ref[w_tile(row, lane), :].astype(F32)
                    there = wb_ref[w_tile(row, lane), :].astype(F32)
                    tile = jnp.where(core0, there, here) if half else jnp.where(core0, here, there)
                    mu = half * HALF + row
                    above = (c16 + lane) - (r16 + mu)
                    at = (slice(mu, mu + 16), slice(lane, lane + 128))
                    if lane // BLK >= mu // BLK:
                        re_ref[at] = jnp.where(above >= 0, tile, 0.0).astype(BF)
                    if lane // BLK <= mu // BLK:
                        im_ref[at] = jnp.where(above < 0, tile, 0.0).astype(BF)
        acc_ref[...] = jnp.zeros_like(acc_ref)

    p = [p_ref[s] for s in range(BATCH)]
    wide = jnp.concatenate(p, axis=1)
    acc = acc_ref[...]
    for blk in range(NB):
        a, b = blk * BLK, blk * BLK + BLK
        re = dot(re_ref[a:b, a:NAUX], wide[a:NAUX]).astype(BF)
        im = dot(im_ref[a:b, 0:b], wide[0:b]).astype(BF)
        for s in range(BATCH):
            lanes = slice(s * 128, s * 128 + 128)
            acc += lax.dot_general(
                p[s][a:b],
                jnp.concatenate([re[:, lanes], im[:, lanes]], axis=1),
                (((0,), (0,)), ((), ())),
                preferred_element_type=F32,
            )
    acc_ref[...] = acc

    @pl.when(step == pl.num_programs(0) - 1)
    def _():
        yi = acc_ref[:, 128:256]
        low = lax.broadcasted_iota(jnp.int32, yi.shape, 1) < BANDS
        turned = pltpu.roll(yi, BANDS, 1)
        y = acc_ref[:, 0:128] + jnp.where(low, -turned, turned)
        z = y + y.T
        re = z[:BANDS, :BANDS] + z[BANDS:, BANDS:]
        im = z[:BANDS, BANDS:] - z[BANDS:, :BANDS]
        sig_ref[...] = PREFACTOR * jnp.concatenate([re, im], axis=1)
        h = s_ref[0]
        rows = BANDS // 2
        keep_ref[...] = sig_ref[pl.ds(pl.multiple_of(h * rows, rows), rows), :]
        send_ref[...] = sig_ref[pl.ds(pl.multiple_of((1 - h) * rows, rows), rows), :]


def screened_sigma(h, core, products, here, there):
    rows = BANDS // 2
    part = jax.ShapeDtypeStruct((rows, 2 * BANDS), F32)
    return pl.pallas_call(
        sigma_kernel,
        out_shape=(part, part),
        grid=(OCC // BATCH,),
        in_specs=[
            pl.BlockSpec(memory_space=pltpu.SMEM),
            pl.BlockSpec((BATCH, NAUX, 128), lambda i: (i, 0, 0)),
            pl.BlockSpec(memory_space=pltpu.VMEM),
            pl.BlockSpec(memory_space=pltpu.VMEM),
        ],
        out_specs=(whole((rows, 2 * BANDS)),) * 2,
        scratch_shapes=[
            pltpu.VMEM((NAUX, NAUX), BF),
            pltpu.VMEM((NAUX, NAUX), BF),
            pltpu.VMEM((128, 256), F32),
            pltpu.VMEM((BANDS, 128), F32),
        ],
        compiler_params=params(24),
        name="screened_sigma",
    )(jnp.stack([h, core]), products, here, there)


def place(k):
    return k % 2 * (PEERS // 2) + k // 2


def by_core(ids):
    return place(ids).reshape(PEERS // 2, 2).T.reshape(PEERS)


def params(mib):
    return pltpu.CompilerParams(vmem_limit_bytes=mib * 2**20)


def whole(shape):
    return pl.BlockSpec(shape, lambda i, *_: (0,) * len(shape))


def x_crossing():
    ids = np.arange(8 * 2 * 4 * 2 * 2).reshape(8, 2, 4, 2, 2)
    pairs = []
    for z, xl, y, core, aux in np.ndindex(ids.shape):
        pairs.append((int(ids[z, xl, y, core, aux]), int(ids[z, 1 - xl, y, core, 1 - aux])))
    return pairs


def local(coefficients, triple, neighbors, w_screened, partner, q_ids):
    h = lax.axis_index("aux").astype(jnp.int32)
    me = lax.axis_index(KA).astype(jnp.int32)
    core = lax.axis_index("core").astype(jnp.int32)
    swap = [(0, 1), (1, 0)]
    atoms = triple.shape[0]
    coef = coefficients[0]
    triple = triple.reshape(atoms, 2 * ORBS, AUX_ATOM * ORBS)

    share = atoms // 2
    nbr_other = lax.ppermute(neighbors, "aux", swap)

    smem = pl.BlockSpec(memory_space=pltpu.SMEM)
    vmem = pl.BlockSpec(memory_space=pltpu.VMEM)
    pieces = pl.pallas_call(
        pack_kernel,
        out_shape=jax.ShapeDtypeStruct((PEERS * PIECE, 128), BF),
        in_specs=[smem, vmem, vmem],
        out_specs=vmem,
        compiler_params=params(56),
        name="pack",
    )(h[None], coef, w_screened[0])
    crossed = lax.ppermute(
        lax.dynamic_slice_in_dim(triple, core * share, share), (*KA, "aux"), x_crossing()
    )

    spread = lax.all_to_all(
        pieces.reshape(PEERS, PIECE // 2, 2, 128), BY_CORE, split_axis=0, concat_axis=0, tiled=True
    )
    partner_here = by_core(lax.dynamic_slice_in_dim(partner, h, 1, 0)[0])
    partner_here, q_place, nbr_other = lax.optimization_barrier(
        (partner_here, place(q_ids), nbr_other)
    )
    split = FAR_ROWS // 2

    def own_piece(t):
        return lax.dynamic_slice(spread, (q_place[t], split, 0, 0), (1, W_ROWS // 2, 2, 128))

    got = lax.ppermute(own_piece(1 - h), "aux", swap)
    routed = pl.pallas_call(
        route_kernel,
        out_shape=jax.ShapeDtypeStruct(spread.shape, BF),
        in_specs=[smem, smem, vmem, vmem, vmem],
        out_specs=vmem,
        compiler_params=params(12),
        name="route",
    )(h[None], partner_here, spread, own_piece(h), got)
    arrived = lax.all_to_all(routed, BY_CORE, split_axis=0, concat_axis=0, tiled=True)

    here = arrived[:, split:].reshape(PACKED, 128)
    far = arrived[:, :split].reshape(FAR, 128)
    here, far = lax.optimization_barrier((here, far))
    there = lax.ppermute(here, "core", swap)
    others = (1 - h) * atoms
    products, x, own_done = pair_products(h * atoms, neighbors, far, [triple], coef, mib=OWN_MIB)
    crossed, own_done = lax.optimization_barrier((crossed, own_done))
    crossed2 = lax.ppermute(crossed, "core", swap)
    near, away = core * share, (1 - core) * share
    products = pair_products(
        others + near, lax.dynamic_slice_in_dim(nbr_other, near, share), x, [crossed], coef, products, own_done
    )
    products = pair_products(
        others + away, lax.dynamic_slice_in_dim(nbr_other, away, share), x, [crossed2], coef, products, own_done
    )
    keep, send = screened_sigma(h, core, products, here, there)
    return (keep + lax.ppermute(send, "aux", swap))[None]


def solution(mesh):
    ka, aux = mesh.devices.shape
    fine = Mesh(mesh.devices.reshape(8, 2, 4, 2, aux), (*KA, "aux"))
    in_specs = (
        P(KA, None, None),
        P("aux", None, None, None),
        P("aux", None),
        P(KA, "aux", None),
        P(),
        P(),
    )
    return jax.shard_map(
        local, mesh=fine, in_specs=in_specs, out_specs=P(KA, "aux", None), check_vma=False
    )
```

```python
import functools
import math

import jax
import jax.numpy as jnp
import numpy as np
from jax import lax
from jax.experimental import pallas as pl
from jax.experimental.pallas import tpu as pltpu
from jax.sharding import Mesh
from jax.sharding import PartitionSpec as P

ATOMS = 64
ORBS = 64
AUX_ATOM = 12
BANDS = 64
OCC = 16
TRANSFERS = 2
NAUX = ATOMS * AUX_ATOM
HALF = NAUX // 2
BF = jnp.bfloat16
F32 = jnp.float32
KA = ("z", "xl", "y", "core")
BY_CORE = ("core", "z", "xl", "y")
PEERS = 128
FAR = 2 * OCC * ATOMS * ORBS // 128
FAR_ROWS = FAR // PEERS
PACKED = HALF * NAUX // 128
W_ROWS = PACKED // PEERS
PIECE = FAR_ROWS + W_ROWS
PREFACTOR = -1.0 / math.sqrt(TRANSFERS * NAUX * OCC)


def dot(a, b):
    return jnp.dot(a, b, preferred_element_type=F32)


def w_tile(row, lane):
    at = (row // 16 * (NAUX // 128) + lane // 128) * 16
    return slice(at, at + 16)


def pack_kernel(h_ref, c_ref, w_ref, out_ref):
    y = lax.broadcasted_iota(jnp.int32, (2 * OCC, 128), 0)
    col = lax.broadcasted_iota(jnp.int32, (2 * OCC, 128), 1)
    pick = (col == jnp.where(y < OCC, y, y + BANDS - OCC)).astype(F32).astype(BF)
    for ob in range(ATOMS // 2):
        far = lax.dot_general(
            pick,
            c_ref[ob * 128 : (ob + 1) * 128, :],
            (((1,), (1,)), ((), ())),
            preferred_element_type=F32,
        )
        for i in range(4):
            at = (4 * ob + i) * PIECE
            out_ref[at : at + FAR_ROWS, :] = far[i * 8 : i * 8 + 8].astype(BF)
    row0 = h_ref[0] * HALF
    r16 = lax.broadcasted_iota(jnp.int32, (16, 128), 0)
    c16 = lax.broadcasted_iota(jnp.int32, (16, 128), 1)
    for row in range(0, HALF, 16):
        for lane in range(0, NAUX, 128):
            above = (c16 + lane) - (r16 + row) - row0
            rows = slice(row, row + 16)
            wr = w_ref[rows, lane : lane + 128].astype(F32)
            wi = w_ref[rows, NAUX + lane : NAUX + lane + 128].astype(F32)
            packed = jnp.where(above > 0, wr, jnp.where(above == 0, 0.5 * wr, wi))
            packed = packed.astype(BF)
            tile = w_tile(row, lane)
            a = tile.start
            while a < tile.stop:
                piece, at = divmod(a, W_ROWS)
                b = min(tile.stop, a - at + W_ROWS)
                to = piece * PIECE + FAR_ROWS + at
                out_ref[to : to + b - a, :] = packed[a - tile.start : b - tile.start]
                a = b


def share_kernel(first_ref, triple_ref, out_ref, stage_ref, in_sem, out_sem):
    parts = in_sem.shape[0]
    size = out_ref.shape[0] // parts
    reads, writes = [], []
    for n in range(parts):
        rows = pl.ds(n * size, size)
        source = triple_ref.at[pl.ds(first_ref[0] + n * size, size)]
        reads.append(pltpu.make_async_copy(source, stage_ref.at[rows], in_sem.at[n]))
        writes.append(pltpu.make_async_copy(stage_ref.at[rows], out_ref.at[rows], out_sem.at[n]))
    for copy in reads:
        copy.start()
    for read, write in zip(reads, writes):
        read.wait()
        write.start()
    for copy in writes:
        copy.wait()


def route_kernel(h_ref, partner_ref, r_ref, own_ref, got_ref, out_ref):
    split = FAR_ROWS // 2
    first = h_ref[0] == 0

    def fill(halves):
        for k in range(PEERS):
            out_ref[k, split:] = halves[k // (PEERS // 2)][0]

    pl.when(first)(lambda: fill((own_ref, got_ref)))
    pl.when(jnp.logical_not(first))(lambda: fill((got_ref, own_ref)))
    for k in range(PEERS):
        out_ref[k, 0:split] = r_ref[partner_ref[k], 0:split]


OWN_MIB = 48
OTHER_MIB = 24
GROUP = 8
GROUP_AUX = GROUP * AUX_ATOM
PITCH = GROUP_AUX + 1


def spread_far(far_ref, x_ref):
    low32 = lax.broadcasted_iota(jnp.int32, (2 * OCC, 128), 1) < ORBS
    for ob in range(ATOMS // 2):
        tops = [(4 * ob + i) * FAR_ROWS for i in range(4)]
        both = jnp.concatenate([far_ref[a : a + FAR_ROWS, :].astype(F32) for a in tops], axis=0)
        turned = pltpu.roll(both, 64, 1)
        x_ref[2 * ob] = jnp.where(low32, both, turned).astype(BF)
        x_ref[2 * ob + 1] = jnp.where(low32, turned, both).astype(BF)


def pair_kernel(s_ref, nbr_ref, far_ref, x_ref, triple_refs, coef_ref, out_ref, stage_ref, c_ref, w_ref, p_ref, sems):
    step = pl.program_id(0)
    low32 = lax.broadcasted_iota(jnp.int32, (2 * OCC, 128), 1) < ORBS

    count = stage_ref.shape[0]
    steps = count // GROUP
    each = steps // len(triple_refs)

    def fetch(n):
        source = triple_refs[n // each].at[pl.ds(n % each * GROUP, GROUP)]
        return pltpu.make_async_copy(source, stage_ref.at[pl.ds(n * GROUP, GROUP)], sems.at[n])

    def fetch_own():
        rows = pl.ds(pl.multiple_of(s_ref[0] * ORBS, ORBS), c_ref.shape[0])
        return pltpu.make_async_copy(coef_ref.at[rows], c_ref, sems.at[sems.shape[0] - 1])

    @pl.when(step == 0)
    def _():
        fetch(0).start()
        fetch_own().start()
        for n in range(1, steps):
            fetch(n).start()
        w_ref[...] = jnp.zeros_like(w_ref)
        if far_ref is not None:
            spread_far(far_ref, x_ref)
        fetch_own().wait()

    for n in range(steps):
        pl.when(step == n)(fetch(n).wait)
    first_at = step * GROUP
    for g in range(GROUP):
        at = first_at + g
        n0 = nbr_ref[at, 0]
        n1 = nbr_ref[at, 1]
        lhs = jnp.where(low32, x_ref[n0].astype(F32), x_ref[n1].astype(F32)).astype(BF)
        pair = dot(lhs, stage_ref[step * GROUP + g]).astype(BF)
        own = c_ref[pl.ds(pl.multiple_of(at * ORBS, ORBS), ORBS), :].astype(F32)
        sign = jnp.where(lax.broadcasted_iota(jnp.int32, own.shape, 1) < BANDS, 1.0, -1.0)
        first = (own * sign).astype(BF)
        second = pltpu.roll(own, BANDS, 1).astype(BF)
        w_ref[g, 0:64, 0:128] = first
        w_ref[g, 64:128, 128:256] = first
        w_ref[g, 128:192, 0:128] = second
        w_ref[g, 192:256, 128:256] = second
        left = jnp.concatenate(
            [
                jnp.concatenate(
                    [pair[0:16, q * 128 : q * 128 + 128], pair[16:32, q * 128 : q * 128 + 128]],
                    axis=1,
                )
                for q in range(AUX_ATOM // 2)
            ],
            axis=0,
        )
        prod = dot(left, w_ref[g])
        for q in range(AUX_ATOM // 2):
            for e in range(2):
                mu = g * AUX_ATOM + 2 * q + e
                for s in range(2):
                    p_ref[pl.ds(mu + s * 8 * PITCH, 8, stride=PITCH), :] = prod[
                        q * 16 + s * 8 : q * 16 + s * 8 + 8, e * 128 : e * 128 + 128
                    ]

    rows = pl.ds(pl.multiple_of(first_at * AUX_ATOM, GROUP_AUX), GROUP_AUX)
    for l in range(OCC):
        out_ref[l, rows, :] = p_ref[l * PITCH : l * PITCH + GROUP_AUX, :].astype(BF)


def pair_products(first, nbr, x, triples, coef, into=None, after=None, mib=24):
    count = sum(t.shape[0] for t in triples)
    m = len(triples)
    extra = () if into is None else (into, after)

    def kernel(s_ref, nbr_ref, x_ref, *rest):
        triple_refs, coef_ref, rest = rest[:m], rest[m], rest[m + 1 :]
        if extra:
            pair_kernel(s_ref, nbr_ref, None, x_ref, triple_refs, coef_ref, *rest[2:])
        else:
            out_ref, made_ref, done_ref, *scratch = rest
            done_ref[...] = jnp.zeros_like(done_ref)
            pair_kernel(s_ref, nbr_ref, x_ref, made_ref, triple_refs, coef_ref, out_ref, *scratch)

    vmem = pl.BlockSpec(memory_space=pltpu.VMEM)
    out_shape = jax.ShapeDtypeStruct((OCC, NAUX, 128), BF)
    out_spec = pl.BlockSpec((OCC, count * AUX_ATOM, 128), lambda i, s, _: (0, s[0] // count, 0))
    made = jax.ShapeDtypeStruct((ATOMS, 2 * OCC, 128), BF)
    token = jax.ShapeDtypeStruct((8, 128), F32)
    return pl.pallas_call(
        kernel,
        out_shape=out_shape if extra else (out_shape, made, token),
        grid_spec=pltpu.PrefetchScalarGridSpec(
            num_scalar_prefetch=2,
            grid=(count // GROUP,),
            in_specs=[
                whole(made.shape) if extra else vmem,
                *(pl.BlockSpec(memory_space=pltpu.HBM) for _ in (*triples, coef)),
                *(pl.BlockSpec(memory_space=pl.ANY) for _ in extra),
            ],
            out_specs=out_spec if extra else (out_spec, whole(made.shape), whole(token.shape)),
            scratch_shapes=[
                pltpu.VMEM((count, *triples[0].shape[1:]), BF),
                pltpu.VMEM((count * ORBS, 128), BF),
                pltpu.VMEM((GROUP, 256, 256), BF),
                pltpu.VMEM((OCC * PITCH + 8, 128), F32),
                pltpu.SemaphoreType.DMA((count // GROUP + 1,)),
            ],
        ),
        input_output_aliases={m + 4: 0} if extra else {},
        compiler_params=params(mib),
        cost_estimate=pl.CostEstimate(
            flops=count * 200_000_000, bytes_accessed=count * 250_000, transcendentals=0
        ),
        name="pair_products",
    )(first[None], nbr, x, *triples, coef, *extra)


BLK = 256
NB = NAUX // BLK
BATCH = 16


def sigma_kernel(s_ref, p_ref, wa_ref, wb_ref, keep_ref, send_ref, re_ref, im_ref, acc_ref, sig_ref):
    step = pl.program_id(0)

    @pl.when(step == 0)
    def _():
        core0 = s_ref[1] == 0
        r16 = lax.broadcasted_iota(jnp.int32, (16, 128), 0)
        c16 = lax.broadcasted_iota(jnp.int32, (16, 128), 1)
        for half in range(2):
            for row in range(0, HALF, 16):
                for lane in range(0, NAUX, 128):
                    here = wa_ref[w_tile(row, lane), :].astype(F32)
                    there = wb_ref[w_tile(row, lane), :].astype(F32)
                    tile = jnp.where(core0, there, here) if half else jnp.where(core0, here, there)
                    mu = half * HALF + row
                    above = (c16 + lane) - (r16 + mu)
                    at = (slice(mu, mu + 16), slice(lane, lane + 128))
                    if lane // BLK >= mu // BLK:
                        re_ref[at] = jnp.where(above >= 0, tile, 0.0).astype(BF)
                    if lane // BLK <= mu // BLK:
                        im_ref[at] = jnp.where(above < 0, tile, 0.0).astype(BF)
        acc_ref[...] = jnp.zeros_like(acc_ref)

    p = [p_ref[s] for s in range(BATCH)]
    wide = jnp.concatenate(p, axis=1)
    acc = acc_ref[...]
    for blk in range(NB):
        a, b = blk * BLK, blk * BLK + BLK
        re = dot(re_ref[a:b, a:NAUX], wide[a:NAUX]).astype(BF)
        im = dot(im_ref[a:b, 0:b], wide[0:b]).astype(BF)
        for s in range(BATCH):
            lanes = slice(s * 128, s * 128 + 128)
            acc += lax.dot_general(
                p[s][a:b],
                jnp.concatenate([re[:, lanes], im[:, lanes]], axis=1),
                (((0,), (0,)), ((), ())),
                preferred_element_type=F32,
            )
    acc_ref[...] = acc

    @pl.when(step == pl.num_programs(0) - 1)
    def _():
        yi = acc_ref[:, 128:256]
        low = lax.broadcasted_iota(jnp.int32, yi.shape, 1) < BANDS
        turned = pltpu.roll(yi, BANDS, 1)
        y = acc_ref[:, 0:128] + jnp.where(low, -turned, turned)
        z = y + y.T
        re = z[:BANDS, :BANDS] + z[BANDS:, BANDS:]
        im = z[:BANDS, BANDS:] - z[BANDS:, :BANDS]
        sig_ref[...] = PREFACTOR * jnp.concatenate([re, im], axis=1)
        h = s_ref[0]
        rows = BANDS // 2
        keep_ref[...] = sig_ref[pl.ds(pl.multiple_of(h * rows, rows), rows), :]
        send_ref[...] = sig_ref[pl.ds(pl.multiple_of((1 - h) * rows, rows), rows), :]


def screened_sigma(h, core, products, here, there):
    rows = BANDS // 2
    part = jax.ShapeDtypeStruct((rows, 2 * BANDS), F32)
    return pl.pallas_call(
        sigma_kernel,
        out_shape=(part, part),
        grid=(OCC // BATCH,),
        in_specs=[
            pl.BlockSpec(memory_space=pltpu.SMEM),
            pl.BlockSpec((BATCH, NAUX, 128), lambda i: (i, 0, 0)),
            pl.BlockSpec(memory_space=pltpu.VMEM),
            pl.BlockSpec(memory_space=pltpu.VMEM),
        ],
        out_specs=(whole((rows, 2 * BANDS)),) * 2,
        scratch_shapes=[
            pltpu.VMEM((NAUX, NAUX), BF),
            pltpu.VMEM((NAUX, NAUX), BF),
            pltpu.VMEM((128, 256), F32),
            pltpu.VMEM((BANDS, 128), F32),
        ],
        compiler_params=params(24),
        name="screened_sigma",
    )(jnp.stack([h, core]), products, here, there)


def place(k):
    return k % 2 * (PEERS // 2) + k // 2


def by_core(ids):
    return place(ids).reshape(PEERS // 2, 2).T.reshape(PEERS)


def params(mib):
    return pltpu.CompilerParams(vmem_limit_bytes=mib * 2**20)


def whole(shape):
    return pl.BlockSpec(shape, lambda i, *_: (0,) * len(shape))


def x_crossing():
    ids = np.arange(8 * 2 * 4 * 2 * 2).reshape(8, 2, 4, 2, 2)
    pairs = []
    for z, xl, y, core, aux in np.ndindex(ids.shape):
        pairs.append((int(ids[z, xl, y, core, aux]), int(ids[z, 1 - xl, y, core, 1 - aux])))
    return pairs


def local(coefficients, triple, neighbors, w_screened, partner, q_ids):
    h = lax.axis_index("aux").astype(jnp.int32)
    me = lax.axis_index(KA).astype(jnp.int32)
    core = lax.axis_index("core").astype(jnp.int32)
    swap = [(0, 1), (1, 0)]
    atoms = triple.shape[0]
    coef = coefficients[0]
    triple = triple.reshape(atoms, 2 * ORBS, AUX_ATOM * ORBS)

    share = atoms // 2
    nbr_other = lax.ppermute(neighbors, "aux", swap)

    smem = pl.BlockSpec(memory_space=pltpu.SMEM)
    vmem = pl.BlockSpec(memory_space=pltpu.VMEM)
    pieces = pl.pallas_call(
        pack_kernel,
        out_shape=jax.ShapeDtypeStruct((PEERS * PIECE, 128), BF),
        in_specs=[smem, vmem, vmem],
        out_specs=vmem,
        compiler_params=params(56),
        name="pack",
    )(h[None], coef, w_screened[0])
    shared = (share, *triple.shape[1:])
    sent = pl.pallas_call(
        share_kernel,
        out_shape=jax.ShapeDtypeStruct(shared, BF),
        in_specs=[smem, pl.BlockSpec(memory_space=pl.ANY)],
        out_specs=pl.BlockSpec(memory_space=pl.ANY),
        scratch_shapes=[
            pltpu.VMEM(shared, BF),
            pltpu.SemaphoreType.DMA((8,)),
            pltpu.SemaphoreType.DMA((8,)),
        ],
        compiler_params=params(56),
        name="share",
    )((core * share)[None], triple)
    crossed = lax.ppermute(sent, (*KA, "aux"), x_crossing())

    spread = lax.all_to_all(
        pieces.reshape(PEERS, PIECE // 2, 2, 128), BY_CORE, split_axis=0, concat_axis=0, tiled=True
    )
    partner_here = by_core(lax.dynamic_slice_in_dim(partner, h, 1, 0)[0])
    partner_here, q_place, nbr_other = lax.optimization_barrier(
        (partner_here, place(q_ids), nbr_other)
    )
    split = FAR_ROWS // 2

    def own_piece(t):
        return lax.dynamic_slice(spread, (q_place[t], split, 0, 0), (1, W_ROWS // 2, 2, 128))

    got = lax.ppermute(own_piece(1 - h), "aux", swap)
    routed = pl.pallas_call(
        route_kernel,
        out_shape=jax.ShapeDtypeStruct(spread.shape, BF),
        in_specs=[smem, smem, vmem, vmem, vmem],
        out_specs=vmem,
        compiler_params=params(12),
        name="route",
    )(h[None], partner_here, spread, own_piece(h), got)
    arrived = lax.all_to_all(routed, BY_CORE, split_axis=0, concat_axis=0, tiled=True)

    here = arrived[:, split:].reshape(PACKED, 128)
    far = arrived[:, :split].reshape(FAR, 128)
    here, far = lax.optimization_barrier((here, far))
    there = lax.ppermute(here, "core", swap)
    others = (1 - h) * atoms
    products, x, own_done = pair_products(h * atoms, neighbors, far, [triple], coef, mib=OWN_MIB)
    crossed, own_done = lax.optimization_barrier((crossed, own_done))
    crossed2 = lax.ppermute(crossed, "core", swap)
    near, away = core * share, (1 - core) * share
    products = pair_products(
        others + near, lax.dynamic_slice_in_dim(nbr_other, near, share), x, [crossed], coef, products, own_done, mib=OTHER_MIB
    )
    products = pair_products(
        others + away, lax.dynamic_slice_in_dim(nbr_other, away, share), x, [crossed2], coef, products, own_done, mib=OTHER_MIB
    )
    keep, send = screened_sigma(h, core, products, here, there)
    return (keep + lax.ppermute(send, "aux", swap))[None]


def solution(mesh):
    ka, aux = mesh.devices.shape
    fine = Mesh(mesh.devices.reshape(8, 2, 4, 2, aux), (*KA, "aux"))
    in_specs = (
        P(KA, None, None),
        P("aux", None, None, None),
        P("aux", None),
        P(KA, "aux", None),
        P(),
        P(),
    )
    return jax.shard_map(
        local, mesh=fine, in_specs=in_specs, out_specs=P(KA, "aux", None), check_vma=False
    )
```

```python
import functools
import math

import jax
import jax.numpy as jnp
import numpy as np
from jax import lax
from jax.experimental import pallas as pl
from jax.experimental.pallas import tpu as pltpu
from jax.sharding import Mesh
from jax.sharding import PartitionSpec as P

ATOMS = 64
ORBS = 64
AUX_ATOM = 12
BANDS = 64
OCC = 16
TRANSFERS = 2
NAUX = ATOMS * AUX_ATOM
HALF = NAUX // 2
BF = jnp.bfloat16
F32 = jnp.float32
KA = ("z", "xl", "y", "core")
BY_CORE = ("core", "z", "xl", "y")
PEERS = 128
FAR = 2 * OCC * ATOMS * ORBS // 128
FAR_ROWS = FAR // PEERS
PACKED = HALF * NAUX // 128
W_ROWS = PACKED // PEERS
PIECE = FAR_ROWS + W_ROWS
PREFACTOR = -1.0 / math.sqrt(TRANSFERS * NAUX * OCC)


def dot(a, b):
    return jnp.dot(a, b, preferred_element_type=F32)


def w_tile(row, lane):
    at = (row // 16 * (NAUX // 128) + lane // 128) * 16
    return slice(at, at + 16)


def pack_kernel(h_ref, c_ref, w_ref, out_ref):
    y = lax.broadcasted_iota(jnp.int32, (2 * OCC, 128), 0)
    col = lax.broadcasted_iota(jnp.int32, (2 * OCC, 128), 1)
    pick = (col == jnp.where(y < OCC, y, y + BANDS - OCC)).astype(F32).astype(BF)
    for ob in range(ATOMS // 2):
        far = lax.dot_general(
            pick,
            c_ref[ob * 128 : (ob + 1) * 128, :],
            (((1,), (1,)), ((), ())),
            preferred_element_type=F32,
        )
        for i in range(4):
            at = (4 * ob + i) * PIECE
            out_ref[at : at + FAR_ROWS, :] = far[i * 8 : i * 8 + 8].astype(BF)
    row0 = h_ref[0] * HALF
    r16 = lax.broadcasted_iota(jnp.int32, (16, 128), 0)
    c16 = lax.broadcasted_iota(jnp.int32, (16, 128), 1)
    for row in range(0, HALF, 16):
        for lane in range(0, NAUX, 128):
            above = (c16 + lane) - (r16 + row) - row0
            rows = slice(row, row + 16)
            wr = w_ref[rows, lane : lane + 128].astype(F32)
            wi = w_ref[rows, NAUX + lane : NAUX + lane + 128].astype(F32)
            packed = jnp.where(above > 0, wr, jnp.where(above == 0, 0.5 * wr, wi))
            packed = packed.astype(BF)
            tile = w_tile(row, lane)
            a = tile.start
            while a < tile.stop:
                piece, at = divmod(a, W_ROWS)
                b = min(tile.stop, a - at + W_ROWS)
                to = piece * PIECE + FAR_ROWS + at
                out_ref[to : to + b - a, :] = packed[a - tile.start : b - tile.start]
                a = b


def share_kernel(first_ref, triple_ref, out_ref, stage_ref, in_sem, out_sem):
    parts = in_sem.shape[0]
    size = out_ref.shape[0] // parts
    reads, writes = [], []
    for n in range(parts):
        rows = pl.ds(n * size, size)
        source = triple_ref.at[pl.ds(first_ref[0] + n * size, size)]
        reads.append(pltpu.make_async_copy(source, stage_ref.at[rows], in_sem.at[n]))
        writes.append(pltpu.make_async_copy(stage_ref.at[rows], out_ref.at[rows], out_sem.at[n]))
    for copy in reads:
        copy.start()
    for read, write in zip(reads, writes):
        read.wait()
        write.start()
    for copy in writes:
        copy.wait()


def route_kernel(h_ref, partner_ref, r_ref, own_ref, got_ref, out_ref):
    split = FAR_ROWS // 2
    first = h_ref[0] == 0

    def fill(halves):
        for k in range(PEERS):
            out_ref[k, split:] = halves[k // (PEERS // 2)][0]

    pl.when(first)(lambda: fill((own_ref, got_ref)))
    pl.when(jnp.logical_not(first))(lambda: fill((got_ref, own_ref)))
    for k in range(PEERS):
        out_ref[k, 0:split] = r_ref[partner_ref[k], 0:split]


OWN_MIB = 48
OTHER_MIB = 24
GROUP = 4
GROUP_AUX = GROUP * AUX_ATOM
PITCH = GROUP_AUX + 1


def spread_far(far_ref, x_ref):
    low32 = lax.broadcasted_iota(jnp.int32, (2 * OCC, 128), 1) < ORBS
    for ob in range(ATOMS // 2):
        tops = [(4 * ob + i) * FAR_ROWS for i in range(4)]
        both = jnp.concatenate([far_ref[a : a + FAR_ROWS, :].astype(F32) for a in tops], axis=0)
        turned = pltpu.roll(both, 64, 1)
        x_ref[2 * ob] = jnp.where(low32, both, turned).astype(BF)
        x_ref[2 * ob + 1] = jnp.where(low32, turned, both).astype(BF)


def pair_kernel(s_ref, nbr_ref, far_ref, x_ref, triple_refs, coef_ref, out_ref, stage_ref, c_ref, w_ref, p_ref, sems):
    step = pl.program_id(0)
    low32 = lax.broadcasted_iota(jnp.int32, (2 * OCC, 128), 1) < ORBS

    count = stage_ref.shape[0]
    steps = count // GROUP
    each = steps // len(triple_refs)

    def fetch(n):
        source = triple_refs[n // each].at[pl.ds(n % each * GROUP, GROUP)]
        return pltpu.make_async_copy(source, stage_ref.at[pl.ds(n * GROUP, GROUP)], sems.at[n])

    def fetch_own():
        rows = pl.ds(pl.multiple_of(s_ref[0] * ORBS, ORBS), c_ref.shape[0])
        return pltpu.make_async_copy(coef_ref.at[rows], c_ref, sems.at[sems.shape[0] - 1])

    @pl.when(step == 0)
    def _():
        fetch(0).start()
        fetch_own().start()
        for n in range(1, steps):
            fetch(n).start()
        w_ref[...] = jnp.zeros_like(w_ref)
        if far_ref is not None:
            spread_far(far_ref, x_ref)
        fetch_own().wait()

    for n in range(steps):
        pl.when(step == n)(fetch(n).wait)
    first_at = step * GROUP
    for g in range(GROUP):
        at = first_at + g
        n0 = nbr_ref[at, 0]
        n1 = nbr_ref[at, 1]
        lhs = jnp.where(low32, x_ref[n0].astype(F32), x_ref[n1].astype(F32)).astype(BF)
        pair = dot(lhs, stage_ref[step * GROUP + g]).astype(BF)
        own = c_ref[pl.ds(pl.multiple_of(at * ORBS, ORBS), ORBS), :].astype(F32)
        sign = jnp.where(lax.broadcasted_iota(jnp.int32, own.shape, 1) < BANDS, 1.0, -1.0)
        first = (own * sign).astype(BF)
        second = pltpu.roll(own, BANDS, 1).astype(BF)
        w_ref[g, 0:64, 0:128] = first
        w_ref[g, 64:128, 128:256] = first
        w_ref[g, 128:192, 0:128] = second
        w_ref[g, 192:256, 128:256] = second
        left = jnp.concatenate(
            [
                jnp.concatenate(
                    [pair[0:16, q * 128 : q * 128 + 128], pair[16:32, q * 128 : q * 128 + 128]],
                    axis=1,
                )
                for q in range(AUX_ATOM // 2)
            ],
            axis=0,
        )
        prod = dot(left, w_ref[g])
        for q in range(AUX_ATOM // 2):
            for e in range(2):
                mu = g * AUX_ATOM + 2 * q + e
                for s in range(2):
                    p_ref[pl.ds(mu + s * 8 * PITCH, 8, stride=PITCH), :] = prod[
                        q * 16 + s * 8 : q * 16 + s * 8 + 8, e * 128 : e * 128 + 128
                    ]

    rows = pl.ds(pl.multiple_of(first_at * AUX_ATOM, GROUP_AUX), GROUP_AUX)
    for l in range(OCC):
        out_ref[l, rows, :] = p_ref[l * PITCH : l * PITCH + GROUP_AUX, :].astype(BF)


def pair_products(first, nbr, x, triples, coef, into=None, after=None, mib=24):
    count = sum(t.shape[0] for t in triples)
    m = len(triples)
    extra = () if into is None else (into, after)

    def kernel(s_ref, nbr_ref, x_ref, *rest):
        triple_refs, coef_ref, rest = rest[:m], rest[m], rest[m + 1 :]
        if extra:
            pair_kernel(s_ref, nbr_ref, None, x_ref, triple_refs, coef_ref, *rest[2:])
        else:
            out_ref, made_ref, done_ref, *scratch = rest
            done_ref[...] = jnp.zeros_like(done_ref)
            pair_kernel(s_ref, nbr_ref, x_ref, made_ref, triple_refs, coef_ref, out_ref, *scratch)

    vmem = pl.BlockSpec(memory_space=pltpu.VMEM)
    out_shape = jax.ShapeDtypeStruct((OCC, NAUX, 128), BF)
    out_spec = pl.BlockSpec((OCC, count * AUX_ATOM, 128), lambda i, s, _: (0, s[0] // count, 0))
    made = jax.ShapeDtypeStruct((ATOMS, 2 * OCC, 128), BF)
    token = jax.ShapeDtypeStruct((8, 128), F32)
    return pl.pallas_call(
        kernel,
        out_shape=out_shape if extra else (out_shape, made, token),
        grid_spec=pltpu.PrefetchScalarGridSpec(
            num_scalar_prefetch=2,
            grid=(count // GROUP,),
            in_specs=[
                whole(made.shape) if extra else vmem,
                *(pl.BlockSpec(memory_space=pltpu.HBM) for _ in (*triples, coef)),
                *(pl.BlockSpec(memory_space=pl.ANY) for _ in extra),
            ],
            out_specs=out_spec if extra else (out_spec, whole(made.shape), whole(token.shape)),
            scratch_shapes=[
                pltpu.VMEM((count, *triples[0].shape[1:]), BF),
                pltpu.VMEM((count * ORBS, 128), BF),
                pltpu.VMEM((GROUP, 256, 256), BF),
                pltpu.VMEM((OCC * PITCH + 8, 128), F32),
                pltpu.SemaphoreType.DMA((count // GROUP + 1,)),
            ],
        ),
        input_output_aliases={m + 4: 0} if extra else {},
        compiler_params=params(mib),
        cost_estimate=pl.CostEstimate(
            flops=count * 200_000_000, bytes_accessed=count * 250_000, transcendentals=0
        ),
        name="pair_products",
    )(first[None], nbr, x, *triples, coef, *extra)


BLK = 256
NB = NAUX // BLK
BATCH = 16


def sigma_kernel(s_ref, p_ref, wa_ref, wb_ref, keep_ref, send_ref, re_ref, im_ref, acc_ref, sig_ref):
    step = pl.program_id(0)

    @pl.when(step == 0)
    def _():
        core0 = s_ref[1] == 0
        r16 = lax.broadcasted_iota(jnp.int32, (16, 128), 0)
        c16 = lax.broadcasted_iota(jnp.int32, (16, 128), 1)
        for half in range(2):
            for row in range(0, HALF, 16):
                for lane in range(0, NAUX, 128):
                    here = wa_ref[w_tile(row, lane), :].astype(F32)
                    there = wb_ref[w_tile(row, lane), :].astype(F32)
                    tile = jnp.where(core0, there, here) if half else jnp.where(core0, here, there)
                    mu = half * HALF + row
                    above = (c16 + lane) - (r16 + mu)
                    at = (slice(mu, mu + 16), slice(lane, lane + 128))
                    if lane // BLK >= mu // BLK:
                        re_ref[at] = jnp.where(above >= 0, tile, 0.0).astype(BF)
                    if lane // BLK <= mu // BLK:
                        im_ref[at] = jnp.where(above < 0, tile, 0.0).astype(BF)
        acc_ref[...] = jnp.zeros_like(acc_ref)

    p = [p_ref[s] for s in range(BATCH)]
    wide = jnp.concatenate(p, axis=1)
    acc = acc_ref[...]
    for blk in range(NB):
        a, b = blk * BLK, blk * BLK + BLK
        re = dot(re_ref[a:b, a:NAUX], wide[a:NAUX]).astype(BF)
        im = dot(im_ref[a:b, 0:b], wide[0:b]).astype(BF)
        for s in range(BATCH):
            lanes = slice(s * 128, s * 128 + 128)
            acc += lax.dot_general(
                p[s][a:b],
                jnp.concatenate([re[:, lanes], im[:, lanes]], axis=1),
                (((0,), (0,)), ((), ())),
                preferred_element_type=F32,
            )
    acc_ref[...] = acc

    @pl.when(step == pl.num_programs(0) - 1)
    def _():
        yi = acc_ref[:, 128:256]
        low = lax.broadcasted_iota(jnp.int32, yi.shape, 1) < BANDS
        turned = pltpu.roll(yi, BANDS, 1)
        y = acc_ref[:, 0:128] + jnp.where(low, -turned, turned)
        z = y + y.T
        re = z[:BANDS, :BANDS] + z[BANDS:, BANDS:]
        im = z[:BANDS, BANDS:] - z[BANDS:, :BANDS]
        sig_ref[...] = PREFACTOR * jnp.concatenate([re, im], axis=1)
        h = s_ref[0]
        rows = BANDS // 2
        keep_ref[...] = sig_ref[pl.ds(pl.multiple_of(h * rows, rows), rows), :]
        send_ref[...] = sig_ref[pl.ds(pl.multiple_of((1 - h) * rows, rows), rows), :]


def screened_sigma(h, core, products, here, there):
    rows = BANDS // 2
    part = jax.ShapeDtypeStruct((rows, 2 * BANDS), F32)
    return pl.pallas_call(
        sigma_kernel,
        out_shape=(part, part),
        grid=(OCC // BATCH,),
        in_specs=[
            pl.BlockSpec(memory_space=pltpu.SMEM),
            pl.BlockSpec((BATCH, NAUX, 128), lambda i: (i, 0, 0)),
            pl.BlockSpec(memory_space=pltpu.VMEM),
            pl.BlockSpec(memory_space=pltpu.VMEM),
        ],
        out_specs=(whole((rows, 2 * BANDS)),) * 2,
        scratch_shapes=[
            pltpu.VMEM((NAUX, NAUX), BF),
            pltpu.VMEM((NAUX, NAUX), BF),
            pltpu.VMEM((128, 256), F32),
            pltpu.VMEM((BANDS, 128), F32),
        ],
        compiler_params=params(24),
        name="screened_sigma",
    )(jnp.stack([h, core]), products, here, there)


def place(k):
    return k % 2 * (PEERS // 2) + k // 2


def by_core(ids):
    return place(ids).reshape(PEERS // 2, 2).T.reshape(PEERS)


def params(mib):
    return pltpu.CompilerParams(vmem_limit_bytes=mib * 2**20)


def whole(shape):
    return pl.BlockSpec(shape, lambda i, *_: (0,) * len(shape))


def x_crossing():
    ids = np.arange(8 * 2 * 4 * 2 * 2).reshape(8, 2, 4, 2, 2)
    pairs = []
    for z, xl, y, core, aux in np.ndindex(ids.shape):
        pairs.append((int(ids[z, xl, y, core, aux]), int(ids[z, 1 - xl, y, core, 1 - aux])))
    return pairs


def local(coefficients, triple, neighbors, w_screened, partner, q_ids):
    h = lax.axis_index("aux").astype(jnp.int32)
    me = lax.axis_index(KA).astype(jnp.int32)
    core = lax.axis_index("core").astype(jnp.int32)
    swap = [(0, 1), (1, 0)]
    atoms = triple.shape[0]
    coef = coefficients[0]
    triple = triple.reshape(atoms, 2 * ORBS, AUX_ATOM * ORBS)

    share = atoms // 2
    nbr_other = lax.ppermute(neighbors, "aux", swap)

    smem = pl.BlockSpec(memory_space=pltpu.SMEM)
    vmem = pl.BlockSpec(memory_space=pltpu.VMEM)
    pieces = pl.pallas_call(
        pack_kernel,
        out_shape=jax.ShapeDtypeStruct((PEERS * PIECE, 128), BF),
        in_specs=[smem, vmem, vmem],
        out_specs=vmem,
        compiler_params=params(56),
        name="pack",
    )(h[None], coef, w_screened[0])
    shared = (share, *triple.shape[1:])
    sent = pl.pallas_call(
        share_kernel,
        out_shape=jax.ShapeDtypeStruct(shared, BF),
        in_specs=[smem, pl.BlockSpec(memory_space=pl.ANY)],
        out_specs=pl.BlockSpec(memory_space=pl.ANY),
        scratch_shapes=[
            pltpu.VMEM(shared, BF),
            pltpu.SemaphoreType.DMA((8,)),
            pltpu.SemaphoreType.DMA((8,)),
        ],
        compiler_params=params(56),
        name="share",
    )((core * share)[None], triple)
    crossed = lax.ppermute(sent, (*KA, "aux"), x_crossing())

    spread = lax.all_to_all(
        pieces.reshape(PEERS, PIECE // 2, 2, 128), BY_CORE, split_axis=0, concat_axis=0, tiled=True
    )
    partner_here = by_core(lax.dynamic_slice_in_dim(partner, h, 1, 0)[0])
    partner_here, q_place, nbr_other = lax.optimization_barrier(
        (partner_here, place(q_ids), nbr_other)
    )
    split = FAR_ROWS // 2

    def own_piece(t):
        return lax.dynamic_slice(spread, (q_place[t], split, 0, 0), (1, W_ROWS // 2, 2, 128))

    got = lax.ppermute(own_piece(1 - h), "aux", swap)
    routed = pl.pallas_call(
        route_kernel,
        out_shape=jax.ShapeDtypeStruct(spread.shape, BF),
        in_specs=[smem, smem, vmem, vmem, vmem],
        out_specs=vmem,
        compiler_params=params(12),
        name="route",
    )(h[None], partner_here, spread, own_piece(h), got)
    arrived = lax.all_to_all(routed, BY_CORE, split_axis=0, concat_axis=0, tiled=True)

    here = arrived[:, split:].reshape(PACKED, 128)
    far = arrived[:, :split].reshape(FAR, 128)
    here, far = lax.optimization_barrier((here, far))
    there = lax.ppermute(here, "core", swap)
    others = (1 - h) * atoms
    products, x, own_done = pair_products(h * atoms, neighbors, far, [triple], coef, mib=OWN_MIB)
    crossed, own_done = lax.optimization_barrier((crossed, own_done))
    crossed2 = lax.ppermute(crossed, "core", swap)
    near, away = core * share, (1 - core) * share
    products = pair_products(
        others + near, lax.dynamic_slice_in_dim(nbr_other, near, share), x, [crossed], coef, products, own_done, mib=OTHER_MIB
    )
    products = pair_products(
        others + away, lax.dynamic_slice_in_dim(nbr_other, away, share), x, [crossed2], coef, products, own_done, mib=OTHER_MIB
    )
    keep, send = screened_sigma(h, core, products, here, there)
    return (keep + lax.ppermute(send, "aux", swap))[None]


def solution(mesh):
    ka, aux = mesh.devices.shape
    fine = Mesh(mesh.devices.reshape(8, 2, 4, 2, aux), (*KA, "aux"))
    in_specs = (
        P(KA, None, None),
        P("aux", None, None, None),
        P("aux", None),
        P(KA, "aux", None),
        P(),
        P(),
    )
    return jax.shard_map(
        local, mesh=fine, in_specs=in_specs, out_specs=P(KA, "aux", None), check_vma=False
    )
```
